256 devices in a mesh: shot: 16 (over z_lo, y, core), sub: 16 (over x, z_hi).
Axes of the slice: x: 4, y: 4, z: 8 (z_hi: 4, z_lo: 2; z = z_hi * 2 + z_lo), core: 2. Of those that a mesh axis runs over, the one named last changes fastest.
Arguments:
- velocity: float32 [512, 8, 64, 128], P(('shot', 'sub')), may hold values from 0.25 to 0.5
- tile_slot: int32 [512], replicated, may hold values from 0 to 511, each once
- anchors: int32 [16, 2], replicated, may hold values from 0 to 16, as said below
- source_cell: int32 [16], P('shot'), may hold values from 0 to 1048575
- wavelet: float32 [16, 8], P('shot'), may hold values from -24 to 24
- receiver_cells: int32 [16, 256], P('shot'), may hold values from 0 to 1048575
- observed: float32 [16, 8, 256], P('shot'), may hold values from -6 to 6
- fwd_prev: float32 [16, 128, 64, 128], P('shot', 'sub'), may hold values from -6 to 6
- fwd_curr: float32 [16, 128, 64, 128], P('shot', 'sub'), may hold values from -6 to 6
- adj_prev: float32 [16, 128, 64, 128], P('shot', 'sub'), may hold values from -6 to 6
- adj_curr: float32 [16, 128, 64, 128], P('shot', 'sub'), may hold values from -6 to 6
Outputs:
- gradient: float32 [512, 8, 64, 128], P(('shot', 'sub'))
The draws below stay inside these ranges and needn't reach their ends.
Inputs may be any that keep to these rules, and one draw needn't show every extreme that they name: `anchors`: row g is shot g's aperture anchor: a tile index along the first dimension from 0 to 16, then one along the second from 0 to 15.
All inputs are finite; a program needn't handle non-finite values.
Results may differ from the reference program's by a relative error of at most 0.0003.
Values sent between devices are 32-bit elements; how exact they have to be, the bound alone decides.
No kernel may reach another device: no remote copies, remote signals or barrier semaphores. Data moves between devices by JAX's collectives and lax.ppermute only.
A program may use at most 64 MiB of HBM per device.

```python
import jax
import jax.numpy as jnp
from jax import lax

TX = 8
TY = 64
TZ = 128
STEPS = 8
REC = 256
SHOTS = 16
APT = 16
GY = 16
TILES = 512
CELLS = 65536
AX = 128


def draw_anchors(key, part):
    key = jax.random.fold_in(key, 7)
    key_x, key_a, key_b, key_pick = jax.random.split(key, 4)
    along_x = jax.random.randint(key_x, (SHOTS,), 0, APT + 1)
    left_draw = jax.random.randint(key_a, (SHOTS,), 0, SHOTS)
    right_draw = jax.random.randint(key_b, (SHOTS,), 0, SHOTS)
    along_y = left_draw * right_draw // SHOTS
    chosen = jax.random.randint(key_pick, (), 0, SHOTS)
    index = jnp.arange(SHOTS)
    along_x = jnp.where(index == chosen, APT, along_x)
    along_x = jnp.where(index == (chosen + 1) % SHOTS, 0, along_x)
    return jnp.stack([along_x, along_y], axis=1).astype(jnp.int32)


def place_ends(drawn, stream_key, low, high):
    place = [jax.random.randint(jax.random.fold_in(stream_key, axis), (), 0, length) for axis, length in enumerate(drawn.shape)]
    widest = drawn.shape.index(max(drawn.shape))
    beside = place[:widest] + [(place[widest] + 1) % drawn.shape[widest]] + place[widest + 1:]
    return drawn.at[tuple(place)].set(low).at[tuple(beside)].set(high)


def shard_levels(stream_key, shape, shards, least, top_value):
    gain = 1.0
    for position, parts in shards:
        draws = jax.random.uniform(jax.random.fold_in(jax.random.fold_in(stream_key, 6), position), (parts,), jnp.float32, least / len(shards), top_value / len(shards))
        gain = gain * jnp.repeat(jnp.exp(draws), shape[position] // parts).reshape((-1,) + (1,) * (len(shape) - 1 - position))
    return gain


def gaussian(stream_key, shape, spread, most, pieces=(), kind=jnp.bfloat16):
    level = shard_levels(stream_key, shape, pieces, -0.22, 0.18) if pieces else 1.0
    array = jax.random.normal(stream_key, shape, jnp.float32) * spread * level
    return jnp.minimum(jnp.maximum(array, -most), most).astype(kind)


def setup_inputs(seed: int = 0) -> dict:
    splits = jax.random.split(jax.random.key(seed), 12)
    return {
        "velocity": jnp.clip(0.25 + 0.25 * jax.random.uniform(splits[0], (TILES, TX, TY, TZ), jnp.float32) ** shard_levels(splits[0], (TILES, TX, TY, TZ), ((0, 256),), -0.2, 0.2), 0.25, 0.5),
        "tile_slot": jax.random.permutation(splits[1], TILES).astype(jnp.int32),
        "anchors": draw_anchors(jax.random.fold_in(splits[11], 71), 0),
        "source_cell": place_ends(jax.random.randint(splits[3], (SHOTS,), 0, APT * CELLS), jax.random.fold_in(splits[3], 1), 0, (APT * CELLS) - 1).astype(jnp.int32),
        "wavelet": gaussian(splits[4], (SHOTS, STEPS), 4.0, 24.0, ((0, 16),), jnp.float32),
        "receiver_cells": place_ends(jax.random.randint(splits[5], (SHOTS, REC), 0, APT * CELLS), jax.random.fold_in(splits[5], 1), 0, (APT * CELLS) - 1).astype(jnp.int32),
        "observed": gaussian(splits[6], (SHOTS, STEPS, REC), 1.0, 6.0, ((0, 16),), jnp.float32),
        "fwd_prev": gaussian(splits[7], (SHOTS, AX, TY, TZ), 1.0, 6.0, ((0, 16), (1, 16)), jnp.float32),
        "fwd_curr": gaussian(splits[8], (SHOTS, AX, TY, TZ), 1.0, 6.0, ((0, 16), (1, 16)), jnp.float32),
        "adj_prev": gaussian(splits[9], (SHOTS, AX, TY, TZ), 1.0, 6.0, ((0, 16), (1, 16)), jnp.float32),
        "adj_curr": gaussian(splits[10], (SHOTS, AX, TY, TZ), 1.0, 6.0, ((0, 16), (1, 16)), jnp.float32),
    }


def laplace(wavefield):
    padded = jnp.pad(wavefield, 1)
    summed = padded[2:, 1:-1, 1:-1] + padded[:-2, 1:-1, 1:-1]
    summed = summed + padded[1:-1, 2:, 1:-1] + padded[1:-1, :-2, 1:-1]
    summed = summed + padded[1:-1, 1:-1, 2:] + padded[1:-1, 1:-1, :-2]
    return summed - 6.0 * wavefield


def one_shot(velocity, tile_slot, anchor, source_at, pulses, listeners, recorded, fwd_prev, fwd_curr, adj_prev, adj_curr):
    tile_ids = (anchor[0] + jnp.arange(APT, dtype=jnp.int32)) * GY + anchor[1]
    slots = tile_slot[tile_ids]
    speed = velocity[slots].reshape(AX, TY, TZ)
    speed_sq = speed * speed
    previous, current = fwd_prev, fwd_curr
    laplacians = []
    residuals = []
    for time_step in range(STEPS):
        laplacian = laplace(current)
        advanced = 2.0 * current - previous + speed_sq * laplacian
        advanced = advanced.reshape(-1).at[source_at].add(pulses[time_step]).reshape(AX, TY, TZ)
        residuals.append(advanced.reshape(-1)[listeners] - recorded[time_step])
        laplacians.append(laplacian)
        previous, current = current, advanced
    previous, current = adj_prev, adj_curr
    image_sum = jnp.zeros((AX, TY, TZ), jnp.float32)
    for back_step in range(STEPS):
        advanced = 2.0 * current - previous + speed_sq * laplace(current)
        advanced = advanced.reshape(-1).at[listeners].add(residuals[STEPS - 1 - back_step]).reshape(AX, TY, TZ)
        image_sum = image_sum + speed * advanced * laplacians[STEPS - 1 - back_step]
        previous, current = current, advanced
    shot_gradient = (2.0 / STEPS) * image_sum
    return slots, shot_gradient.reshape(APT, TX, TY, TZ)


def reference(velocity, tile_slot, anchors, source_cell, wavelet, receiver_cells, observed, fwd_prev, fwd_curr, adj_prev, adj_curr):
    def visit(gradient, inputs):
        anchor, source_at, pulses, listeners, recorded, f_prev, f_curr, a_prev, a_curr = inputs
        slots, tiles_out = one_shot(velocity, tile_slot, anchor, source_at, pulses, listeners, recorded, f_prev, f_curr, a_prev, a_curr)
        return gradient.at[slots].add(tiles_out), None

    start_grad = jnp.zeros((TILES, TX, TY, TZ), jnp.float32)
    gradient, _ = lax.scan(visit, start_grad, (anchors, source_cell, wavelet, receiver_cells, observed, fwd_prev, fwd_curr, adj_prev, adj_curr))
    return gradient
```

```python
import jax
import jax.numpy as jnp
from jax import lax
from jax.experimental import pallas as pl
from jax.experimental.pallas import tpu as pltpu
from jax.sharding import PartitionSpec as P

ALL = ("shot", "sub")
LANES = 128
STEPS = 8
REC = 256
T = 8
PADY = 8


def split3(x):
    hi = x.astype(jnp.bfloat16)
    rest = x - hi.astype(jnp.float32)
    mid = rest.astype(jnp.bfloat16)
    lo = (rest - mid.astype(jnp.float32)).astype(jnp.bfloat16)
    return hi, mid, lo


def dot3(onehot, x, dims):
    total = None
    for part in reversed(split3(x)):
        term = lax.dot_general(onehot, part, (dims, ((), ())), preferred_element_type=jnp.float32)
        total = term if total is None else total + term
    return total


def pick_kernel(index_ref, x_ref, out_ref):
    rows = x_ref.shape[0]
    index = index_ref[...]
    onehot = (lax.broadcasted_iota(jnp.int32, (rows, index.shape[1]), 0) == index).astype(jnp.bfloat16)
    out_ref[...] = dot3(onehot, x_ref[...], ((0,), (0,)))


def drop_kernel(index_ref, x_ref, out_ref):
    rows = out_ref.shape[0]
    index = index_ref[...]
    onehot = (lax.broadcasted_iota(jnp.int32, (rows, index.shape[1]), 0) == index).astype(jnp.bfloat16)
    out_ref[...] = dot3(onehot, x_ref[...], ((1,), (0,)))


def load_field(dst, low, own, high):
    ny = own.shape[1]
    for block, ref in enumerate((low, own, high)):
        dst[block * T : (block + 1) * T, PADY : PADY + ny, :] = ref[...]


def clear_pad(dst, ny):
    zero = jnp.zeros((dst.shape[0], PADY, LANES), jnp.float32)
    dst[:, 0:PADY, :] = zero
    dst[:, PADY + ny : PADY + ny + PADY, :] = zero


def layer_laplace(cur, x, ny, first, last):
    mid = cur[x, PADY : PADY + ny, :]
    total = cur[x + 1, PADY : PADY + ny, :] + cur[x - 1, PADY : PADY + ny, :]
    total = total + cur[x, PADY + 1 : PADY + 1 + ny, :] + cur[x, PADY - 1 : PADY - 1 + ny, :]
    up = jnp.where(last, 0.0, pltpu.roll(mid, LANES - 1, 1))
    down = jnp.where(first, 0.0, pltpu.roll(mid, 1, 1))
    total = total + up + down
    return mid, total - 6.0 * mid


def forward_kernel(
    src_ref, wave_ref, rec_ref, obs_ref,
    sl, so, sh, pl_, po, ph, cl, co, ch,
    lap_ref, res_ref, prev, cur, speed_sq,
):
    ny = so.shape[1]
    rows = T * ny
    clear_pad(prev, ny)
    clear_pad(cur, ny)
    load_field(prev, pl_, po, ph)
    load_field(cur, cl, co, ch)
    for block, ref in enumerate((sl, so, sh)):
        value = ref[...]
        speed_sq[block * T : (block + 1) * T] = value * value
    lane = lax.broadcasted_iota(jnp.int32, (ny, LANES), 1)
    first, last = lane == 0, lane == LANES - 1
    src_x, src_y, src_z = src_ref[0], src_ref[1], src_ref[2]
    inside = (src_x >= 0) & (src_x < 3 * T)
    src_lane = lax.broadcasted_iota(jnp.int32, (1, LANES), 1) == src_z
    rec = rec_ref[...]
    onehot = (lax.broadcasted_iota(jnp.int32, (rows, REC), 0) == rec[0:1]).astype(jnp.bfloat16)
    z_mask = lax.broadcasted_iota(jnp.int32, (LANES, REC), 0) == rec[1:2]
    own = (rec[0:1] >= 0) & (rec[0:1] < rows)
    for n in range(STEPS):
        old, now = (prev, cur) if n % 2 == 0 else (cur, prev)

        def update(x, keep):
            mid, lap = layer_laplace(now, x, ny, first, last)
            old[x, PADY : PADY + ny, :] = (2.0 * mid - old[x, PADY : PADY + ny, :]) + speed_sq[x] * lap
            return lap

        def outer(x, carry):
            update(x, False)
            return carry

        def inner(x, carry):
            lap_ref[n, x - T] = update(x, True)
            return carry

        lax.fori_loop(1 + n, T, outer, 0)
        lax.fori_loop(T, 2 * T, inner, 0)
        lax.fori_loop(2 * T, 3 * T - 1 - n, outer, 0)

        @pl.when(inside)
        def _():
            row = pl.ds(src_y + PADY, 1)
            old[src_x, row, :] = old[src_x, row, :] + jnp.where(src_lane, wave_ref[n], 0.0)

        field = old[T : 2 * T, PADY : PADY + ny, :].reshape(rows, LANES)
        total = None
        for part in reversed(split3(field)):
            term = lax.dot_general(part, onehot, (((0,), (0,)), ((), ())), preferred_element_type=jnp.float32)
            total = term if total is None else total + term
        sample = jnp.sum(jnp.where(z_mask, total, 0.0), axis=0, keepdims=True)
        res_ref[n : n + 1, :] = jnp.where(own, sample - obs_ref[n : n + 1, :], 0.0)


def adjoint_kernel(
    rec_ref, rl, ro, rh,
    sl, so, sh, pl_, po, ph, cl, co, ch, lap_ref,
    out_ref, prev, cur, speed_sq, inject,
):
    ny = so.shape[1]
    clear_pad(prev, ny)
    clear_pad(cur, ny)
    load_field(prev, pl_, po, ph)
    load_field(cur, cl, co, ch)
    for block, ref in enumerate((sl, so, sh)):
        value = ref[...]
        speed_sq[block * T : (block + 1) * T] = value * value
    lane = lax.broadcasted_iota(jnp.int32, (ny, LANES), 1)
    first, last = lane == 0, lane == LANES - 1
    rec = rec_ref[...]
    resid = rl[...] + ro[...] + rh[...]
    z_mask = lax.broadcasted_iota(jnp.int32, (LANES, REC), 0) == rec[1:2]
    for k in range(STEPS):
        old, now = (prev, cur) if k % 2 == 0 else (cur, prev)
        n = STEPS - 1 - k
        lo, hi = 1 + k, 3 * T - 1 - k
        span = (hi - lo) * ny
        onehot = (
            lax.broadcasted_iota(jnp.int32, (span, REC), 0) == rec[0:1] + (T - lo) * ny
        ).astype(jnp.bfloat16)
        spread = jnp.where(z_mask, resid[n : n + 1, :], 0.0)
        inject[lo:hi] = dot3(onehot, spread, ((1,), (1,))).reshape(hi - lo, ny, LANES)

        def update(x):
            mid, lap = layer_laplace(now, x, ny, first, last)
            new = (2.0 * mid - old[x, PADY : PADY + ny, :]) + speed_sq[x] * lap + inject[x]
            old[x, PADY : PADY + ny, :] = new
            return new

        def outer(x, carry):
            update(x)
            return carry

        def inner(x, carry):
            new = update(x)
            term = so[x - T] * new * lap_ref[n, x - T]
            if k == 0:
                out_ref[x - T] = term
            elif k == STEPS - 1:
                out_ref[x - T] = (2.0 / STEPS) * (out_ref[x - T] + term)
            else:
                out_ref[x - T] = out_ref[x - T] + term
            return carry

        lax.fori_loop(lo, T, outer, 0)
        lax.fori_loop(T, 2 * T, inner, 0)
        lax.fori_loop(2 * T, hi, outer, 0)


def vmem():
    return pl.BlockSpec(memory_space=pltpu.VMEM)


def smem():
    return pl.BlockSpec(memory_space=pltpu.SMEM)


def params():
    return pltpu.CompilerParams(vmem_limit_bytes=48 * 1024 * 1024)


def shards(
    velocity,
    tile_slot,
    anchors,
    source_cell,
    wavelet,
    receiver_cells,
    observed,
    fwd_prev,
    fwd_curr,
    adj_prev,
    adj_curr,
):
    n_shot = lax.axis_size("shot")
    n_sub = lax.axis_size("sub")
    n_all = n_shot * n_sub
    sub_index = lax.axis_index("sub")
    local_slots, layers, ny, nz = velocity.shape
    rows = layers * ny
    piece = rows // n_all
    forward = [(i, i + 1) for i in range(n_sub - 1)]
    backward = [(j, i) for i, j in forward]

    def both(x):
        return lax.ppermute(x, "sub", forward), lax.ppermute(x, "sub", backward)

    tiles = ((anchors[:, 0:1] + jnp.arange(n_sub, dtype=jnp.int32)) * n_shot + anchors[:, 1:2]).reshape(-1)
    table = jnp.arange(tile_slot.shape[0], dtype=jnp.int32)
    wanted = jnp.sum(jnp.where(table[:, None] == tiles[None, :], tile_slot[:, None], 0), axis=0)
    want_rows = (wanted[:, None] * piece + jnp.arange(piece, dtype=jnp.int32)).reshape(1, n_all * piece)

    cells = receiver_cells[0]
    rec = jnp.stack([cells // nz - sub_index * rows, cells % nz])
    src = source_cell[0]
    src_place = jnp.stack([src // (ny * nz) - (sub_index - 1) * layers, src // nz % ny, src % nz])

    with jax.named_scope("spread_velocity"):
        cut = velocity.reshape(local_slots, n_all, piece, nz).transpose(1, 0, 2, 3)
        spread = lax.all_to_all(cut.reshape(n_all, local_slots * piece, nz), ALL, 0, 0, tiled=True)
    with jax.named_scope("pick_velocity"):
        picked = pl.pallas_call(
            pick_kernel,
            out_shape=jax.ShapeDtypeStruct((n_all * piece, nz), jnp.float32),
            in_specs=[vmem(), vmem()],
            out_specs=vmem(),
            compiler_params=params(),
        )(want_rows, spread.reshape(n_all * local_slots * piece, nz))
    with jax.named_scope("deliver_velocity"):
        speed = lax.all_to_all(picked.reshape(n_all, piece, nz), ALL, 0, 0, tiled=True).reshape(layers, ny, nz)

    def triple(x):
        low, high = both(x)
        return low, x, high

    with jax.named_scope("halo_fwd"):
        prev3, cur3 = triple(fwd_prev[0]), triple(fwd_curr[0])
    with jax.named_scope("halo_adj"):
        aprev3, acur3 = triple(adj_prev[0]), triple(adj_curr[0])
    with jax.named_scope("halo_speed"):
        speed3 = triple(speed)

    field = pltpu.VMEM((3 * T, ny + 2 * PADY, nz), jnp.float32)
    flat = pltpu.VMEM((3 * T, ny, nz), jnp.float32)
    with jax.named_scope("forward"):
        laps, resid = pl.pallas_call(
            forward_kernel,
            out_shape=(
                jax.ShapeDtypeStruct((STEPS, layers, ny, nz), jnp.float32),
                jax.ShapeDtypeStruct((STEPS, REC), jnp.float32),
            ),
            in_specs=[smem(), smem()] + [vmem()] * 11,
            out_specs=(vmem(), vmem()),
            scratch_shapes=[field, field, flat],
            compiler_params=params(),
        )(src_place, wavelet[0], rec, observed[0], *speed3, *prev3, *cur3)
    with jax.named_scope("residuals"):
        res3 = triple(resid)
    with jax.named_scope("adjoint"):
        image = pl.pallas_call(
            adjoint_kernel,
            out_shape=jax.ShapeDtypeStruct((layers, ny, nz), jnp.float32),
            in_specs=[vmem()] * 14,
            out_specs=vmem(),
            scratch_shapes=[field, field, flat, flat],
            compiler_params=params(),
        )(rec, *res3, *speed3, *aprev3, *acur3, laps)

    with jax.named_scope("spread_gradient"):
        pieces = lax.all_to_all(image.reshape(n_all, piece, nz), ALL, 0, 0, tiled=True)
    with jax.named_scope("drop_gradient"):
        dropped = pl.pallas_call(
            drop_kernel,
            out_shape=jax.ShapeDtypeStruct((n_all * local_slots * piece, nz), jnp.float32),
            in_specs=[vmem(), vmem()],
            out_specs=vmem(),
            compiler_params=params(),
        )(want_rows, pieces.reshape(n_all * piece, nz))
    with jax.named_scope("deliver_gradient"):
        back = lax.all_to_all(dropped.reshape(n_all, local_slots * piece, nz), ALL, 0, 0, tiled=True)
        back = back.reshape(n_all, local_slots, piece, nz).transpose(1, 0, 2, 3)
    return back.reshape(velocity.shape)


def solution(mesh):
    return jax.shard_map(
        shards,
        mesh=mesh,
        in_specs=(
            P(("shot", "sub"), None, None, None),
            P(),
            P(),
            P("shot"),
            P("shot", None),
            P("shot", None),
            P("shot", None, None),
            P("shot", "sub", None, None),
            P("shot", "sub", None, None),
            P("shot", "sub", None, None),
            P("shot", "sub", None, None),
        ),
        out_specs=P(("shot", "sub"), None, None, None),
        check_vma=False,
    )
```

```python
import jax
import jax.numpy as jnp
from jax import lax
from jax.experimental import pallas as pl
from jax.experimental.pallas import tpu as pltpu
from jax.sharding import PartitionSpec as P

ALL = ("shot", "sub")
LANES = 128
STEPS = 8
REC = 256
T = 8
PADY = 8


def split3(x):
    hi = x.astype(jnp.bfloat16)
    rest = x - hi.astype(jnp.float32)
    mid = rest.astype(jnp.bfloat16)
    lo = (rest - mid.astype(jnp.float32)).astype(jnp.bfloat16)
    return hi, mid, lo


def dot3(onehot, x, dims):
    total = None
    for part in reversed(split3(x)):
        term = lax.dot_general(onehot, part, (dims, ((), ())), preferred_element_type=jnp.float32)
        total = term if total is None else total + term
    return total


def pick_kernel(index_ref, x_ref, out_ref):
    rows = x_ref.shape[0]
    index = index_ref[...]
    onehot = (lax.broadcasted_iota(jnp.int32, (rows, index.shape[1]), 0) == index).astype(jnp.bfloat16)
    out_ref[...] = dot3(onehot, x_ref[...], ((0,), (0,)))


def drop_kernel(index_ref, x_ref, out_ref):
    rows = out_ref.shape[0]
    index = index_ref[...]
    onehot = (lax.broadcasted_iota(jnp.int32, (rows, index.shape[1]), 0) == index).astype(jnp.bfloat16)
    out_ref[...] = dot3(onehot, x_ref[...], ((1,), (0,)))


def each(lo, hi, body):
    for x in range(lo, hi):
        body(x, 0)


def tile_half(speed3, block, half, ny):
    n = T * ny // 2
    value = speed3[pl.ds(2 * block + half, n, stride=6), :]
    return value.reshape(T // 2, ny, LANES)


def square_speed(dst, speed3, ny):
    for block in range(3):
        for half in range(2):
            value = tile_half(speed3, block, half, ny)
            first = block * T + half * (T // 2)
            dst[first : first + T // 2] = value * value


def load_field(dst, edge_ref, low, own, high):
    ny = own.shape[1]
    dst[0:T, PADY : PADY + ny, :] = jnp.where(edge_ref[0] > 0, low[...], 0.0)
    dst[T : 2 * T, PADY : PADY + ny, :] = own[...]
    dst[2 * T : 3 * T, PADY : PADY + ny, :] = jnp.where(edge_ref[1] > 0, high[...], 0.0)


def clear_pad(dst, ny):
    zero = jnp.zeros((dst.shape[0], PADY, LANES), jnp.float32)
    dst[:, 0:PADY, :] = zero
    dst[:, PADY + ny : PADY + ny + PADY, :] = zero


def layer_laplace(cur, x, ny, first, last):
    mid = cur[x, PADY : PADY + ny, :]
    total = cur[x + 1, PADY : PADY + ny, :] + cur[x - 1, PADY : PADY + ny, :]
    total = total + cur[x, PADY + 1 : PADY + 1 + ny, :] + cur[x, PADY - 1 : PADY - 1 + ny, :]
    up = jnp.where(last, 0.0, pltpu.roll(mid, LANES - 1, 1))
    down = jnp.where(first, 0.0, pltpu.roll(mid, 1, 1))
    total = total + up + down
    return mid, total - 6.0 * mid


def forward_kernel(
    edge_ref, src_ref, wave_ref, rec_ref, obs_ref,
    speed3, low, po, co, high,
    lap_ref, res_ref, prev, cur, speed_sq,
):
    ny = po.shape[1]
    rows = T * ny
    clear_pad(prev, ny)
    clear_pad(cur, ny)
    load_field(prev, edge_ref, low.at[0], po, high.at[0])
    load_field(cur, edge_ref, low.at[1], co, high.at[1])
    square_speed(speed_sq, speed3, ny)
    lane = lax.broadcasted_iota(jnp.int32, (ny, LANES), 1)
    first, last = lane == 0, lane == LANES - 1
    src_x, src_y, src_z = src_ref[0], src_ref[1], src_ref[2]
    inside = (src_x >= 0) & (src_x < 3 * T)
    src_lane = lax.broadcasted_iota(jnp.int32, (1, LANES), 1) == src_z
    rec = rec_ref[...]
    onehot = (lax.broadcasted_iota(jnp.int32, (rows, REC), 0) == rec[0:1]).astype(jnp.bfloat16)
    z_mask = lax.broadcasted_iota(jnp.int32, (LANES, REC), 0) == rec[1:2]
    own = (rec[0:1] >= 0) & (rec[0:1] < rows)
    for n in range(STEPS):
        old, now = (prev, cur) if n % 2 == 0 else (cur, prev)

        def update(x, keep):
            mid, lap = layer_laplace(now, x, ny, first, last)
            old[x, PADY : PADY + ny, :] = (2.0 * mid - old[x, PADY : PADY + ny, :]) + speed_sq[x] * lap
            return lap

        def outer(x, carry):
            update(x, False)
            return carry

        def inner(x, carry):
            lap_ref[n, x - T] = update(x, True)
            return carry

        each(1 + n, T, outer)
        each(T, 2 * T, inner)
        each(2 * T, 3 * T - 1 - n, outer)

        @pl.when(inside)
        def _():
            row = pl.ds(src_y + PADY, 1)
            old[src_x, row, :] = old[src_x, row, :] + jnp.where(src_lane, wave_ref[n], 0.0)

        field = old[T : 2 * T, PADY : PADY + ny, :].reshape(rows, LANES)
        total = None
        for part in reversed(split3(field)):
            term = lax.dot_general(part, onehot, (((0,), (0,)), ((), ())), preferred_element_type=jnp.float32)
            total = term if total is None else total + term
        sample = jnp.sum(jnp.where(z_mask, total, 0.0), axis=0, keepdims=True)
        res_ref[n : n + 1, :] = jnp.where(own, sample - obs_ref[n : n + 1, :], 0.0)


def adjoint_kernel(
    edge_ref, rec_ref, rl, ro, rh,
    speed3, low, po, co, high, lap_ref,
    out_ref, prev, cur, speed_sq, inject, speed,
):
    ny = po.shape[1]
    clear_pad(prev, ny)
    clear_pad(cur, ny)
    load_field(prev, edge_ref, low.at[0], po, high.at[0])
    load_field(cur, edge_ref, low.at[1], co, high.at[1])
    square_speed(speed_sq, speed3, ny)
    lane = lax.broadcasted_iota(jnp.int32, (ny, LANES), 1)
    first, last = lane == 0, lane == LANES - 1
    for half in range(2):
        speed[half * (T // 2) : (half + 1) * (T // 2)] = tile_half(speed3, 1, half, ny)
    rec = rec_ref[...]
    resid = rl[...] + ro[...] + rh[...]
    z_mask = lax.broadcasted_iota(jnp.int32, (LANES, REC), 0) == rec[1:2]
    for k in range(STEPS):
        old, now = (prev, cur) if k % 2 == 0 else (cur, prev)
        n = STEPS - 1 - k
        lo, hi = 1 + k, 3 * T - 1 - k
        span = (hi - lo) * ny
        onehot = (
            lax.broadcasted_iota(jnp.int32, (span, REC), 0) == rec[0:1] + (T - lo) * ny
        ).astype(jnp.bfloat16)
        spread = jnp.where(z_mask, resid[n : n + 1, :], 0.0)
        inject[lo:hi] = dot3(onehot, spread, ((1,), (1,))).reshape(hi - lo, ny, LANES)

        def update(x):
            mid, lap = layer_laplace(now, x, ny, first, last)
            new = (2.0 * mid - old[x, PADY : PADY + ny, :]) + speed_sq[x] * lap + inject[x]
            old[x, PADY : PADY + ny, :] = new
            return new

        def outer(x, carry):
            update(x)
            return carry

        def inner(x, carry):
            new = update(x)
            term = speed[x - T] * new * lap_ref[n, x - T]
            if k == 0:
                out_ref[x - T] = term
            elif k == STEPS - 1:
                out_ref[x - T] = (2.0 / STEPS) * (out_ref[x - T] + term)
            else:
                out_ref[x - T] = out_ref[x - T] + term
            return carry

        each(lo, T, outer)
        each(T, 2 * T, inner)
        each(2 * T, hi, outer)


def vmem():
    return pl.BlockSpec(memory_space=pltpu.VMEM)


def smem():
    return pl.BlockSpec(memory_space=pltpu.SMEM)


def params():
    return pltpu.CompilerParams(vmem_limit_bytes=48 * 1024 * 1024)


def call_pick(index, x):
    return pl.pallas_call(
        pick_kernel,
        out_shape=jax.ShapeDtypeStruct((index.shape[1], x.shape[1]), jnp.float32),
        in_specs=[vmem(), vmem()],
        out_specs=vmem(),
        compiler_params=params(),
    )(index, x)


def cut_kernel(x_ref, out_ref):
    k, n, _ = x_ref.shape
    for i in range(k):
        out_ref[pl.ds(i, n, stride=k), :] = x_ref[i]


def call_cut(x):
    return pl.pallas_call(
        cut_kernel,
        out_shape=jax.ShapeDtypeStruct((x.shape[0] * x.shape[1], x.shape[2]), jnp.float32),
        in_specs=[vmem()],
        out_specs=vmem(),
        compiler_params=params(),
    )(x)


def stack_kernel(*refs):
    fields, out, sems = refs[:-2], refs[-2], refs[-1]
    copies = [pltpu.make_async_copy(f, out.at[i], sems.at[i]) for i, f in enumerate(fields)]
    for c in copies:
        c.start()
    for c in copies:
        c.wait()


def call_stack(*fields):
    anywhere = pl.BlockSpec(memory_space=pl.ANY)
    return pl.pallas_call(
        stack_kernel,
        out_shape=jax.ShapeDtypeStruct((len(fields),) + fields[0].shape, jnp.float32),
        in_specs=[anywhere] * len(fields),
        out_specs=anywhere,
        scratch_shapes=[pltpu.SemaphoreType.DMA((len(fields),))],
        compiler_params=params(),
    )(*fields)


def call_forward(edge, src_place, wave, rec, obs, speed3, fields):
    layers, ny, nz = fields[1].shape
    field = pltpu.VMEM((3 * T, ny + 2 * PADY, nz), jnp.float32)
    flat = pltpu.VMEM((3 * T, ny, nz), jnp.float32)
    return pl.pallas_call(
        forward_kernel,
        out_shape=(
            jax.ShapeDtypeStruct((STEPS, layers, ny, nz), jnp.float32),
            jax.ShapeDtypeStruct((STEPS, REC), jnp.float32),
        ),
        in_specs=[smem()] * 3 + [vmem()] * 7,
        out_specs=(vmem(), vmem()),
        scratch_shapes=[field, field, flat],
        compiler_params=params(),
    )(edge, src_place, wave, rec, obs, speed3, *fields)


def call_adjoint(edge, rec, res3, speed3, fields, laps):
    layers, ny, nz = fields[1].shape
    field = pltpu.VMEM((3 * T, ny + 2 * PADY, nz), jnp.float32)
    flat = pltpu.VMEM((3 * T, ny, nz), jnp.float32)
    return pl.pallas_call(
        adjoint_kernel,
        out_shape=jax.ShapeDtypeStruct((layers, ny, nz), jnp.float32),
        in_specs=[smem()] + [vmem()] * 10,
        out_specs=vmem(),
        scratch_shapes=[field, field, flat, flat, pltpu.VMEM((T, ny, nz), jnp.float32)],
        compiler_params=params(),
    )(edge, rec, *res3, speed3, *fields, laps)


def shards(
    velocity,
    tile_slot,
    anchors,
    source_cell,
    wavelet,
    receiver_cells,
    observed,
    fwd_prev,
    fwd_curr,
    adj_prev,
    adj_curr,
):
    n_shot = lax.axis_size("shot")
    n_sub = lax.axis_size("sub")
    n_all = n_shot * n_sub
    sub_index = lax.axis_index("sub")
    local_slots, layers, ny, nz = velocity.shape
    rows = layers * ny
    piece = rows // n_all
    forward = [(i, (i + 1) % n_sub) for i in range(n_sub)]
    backward = [(j, i) for i, j in forward]

    def both(x):
        return lax.ppermute(x, "sub", forward), lax.ppermute(x, "sub", backward)

    tiles = ((anchors[:, 0:1] + jnp.arange(n_sub, dtype=jnp.int32)) * n_shot + anchors[:, 1:2]).reshape(-1)
    table = jnp.arange(tile_slot.shape[0], dtype=jnp.int32)
    wanted = jnp.sum(jnp.where(table[:, None] == tiles[None, :], tile_slot[:, None], 0), axis=0)
    want_rows = (wanted[:, None] * piece + jnp.arange(piece, dtype=jnp.int32)).reshape(1, n_all * piece)

    pad = jnp.pad(wanted.reshape(n_shot, n_sub), ((0, 0), (1, 1)), constant_values=-1)
    near = jnp.stack([pad[:, :-2], pad[:, 1:-1], pad[:, 2:]], axis=-1)
    wide_rows = jnp.where(
        near[..., None] >= 0, near[..., None] * piece + jnp.arange(piece, dtype=jnp.int32), -1
    ).reshape(1, n_all * 3 * piece)
    edge = jnp.stack([sub_index > 0, sub_index < n_sub - 1]).astype(jnp.int32)

    cells = receiver_cells[0]
    rec = jnp.stack([cells // nz - sub_index * rows, cells % nz])
    src = source_cell[0]
    src_place = jnp.stack([src // (ny * nz) - (sub_index - 1) * layers, src // nz % ny, src % nz])

    with jax.named_scope("halo_fields"):
        low, high = both(call_stack(fwd_prev[0], fwd_curr[0]))
        adj_low, adj_high = both(call_stack(adj_prev[0], adj_curr[0]))
    with jax.named_scope("spread_velocity"):
        cut = call_cut(velocity.reshape(local_slots * piece, n_all, nz))
        spread = lax.all_to_all(cut.reshape(n_all, local_slots, piece, nz), ALL, 0, 0, tiled=True)
    with jax.named_scope("pick_velocity"):
        picked = call_pick(wide_rows, spread.reshape(n_all * local_slots * piece, nz))
        picked, low, high = lax.optimization_barrier((picked, low, high))
    with jax.named_scope("deliver_velocity"):
        speed3 = lax.all_to_all(picked.reshape(n_all, 3, piece, nz), ALL, 0, 0, tiled=True)
        speed3 = speed3.reshape(n_all * 3 * piece, nz)

    fwd4 = (low, fwd_prev[0], fwd_curr[0], high)
    adj4 = (adj_low, adj_prev[0], adj_curr[0], adj_high)
    with jax.named_scope("forward"):
        laps, resid = call_forward(edge, src_place, wavelet[0], rec, observed[0], speed3, fwd4)
    with jax.named_scope("residuals"):
        res_low, res_high = both(resid)
        res3 = (res_low, resid, res_high)
    with jax.named_scope("adjoint"):
        image = call_adjoint(edge, rec, res3, speed3, adj4, laps)

    with jax.named_scope("spread_gradient"):
        pieces = lax.all_to_all(image.reshape(n_all, piece, nz), ALL, 0, 0, tiled=True)
    with jax.named_scope("drop_gradient"):
        dropped = pl.pallas_call(
            drop_kernel,
            out_shape=jax.ShapeDtypeStruct((n_all * local_slots * piece, nz), jnp.float32),
            in_specs=[vmem(), vmem()],
            out_specs=vmem(),
            compiler_params=params(),
        )(want_rows, pieces.reshape(n_all * piece, nz))
    with jax.named_scope("deliver_gradient"):
        back = lax.all_to_all(dropped.reshape(n_all, local_slots * piece, nz), ALL, 0, 0, tiled=True)
        back = back.reshape(n_all, local_slots, piece, nz).transpose(1, 0, 2, 3)
    return back.reshape(velocity.shape)


def solution(mesh):
    return jax.shard_map(
        shards,
        mesh=mesh,
        in_specs=(
            P(("shot", "sub"), None, None, None),
            P(),
            P(),
            P("shot"),
            P("shot", None),
            P("shot", None),
            P("shot", None, None),
            P("shot", "sub", None, None),
            P("shot", "sub", None, None),
            P("shot", "sub", None, None),
            P("shot", "sub", None, None),
        ),
        out_specs=P(("shot", "sub"), None, None, None),
        check_vma=False,
    )
```

```python
import functools

import jax
import jax.numpy as jnp
from jax import lax
from jax.experimental import pallas as pl
from jax.experimental.pallas import tpu as pltpu
from jax.sharding import PartitionSpec as P

ALL = ("shot", "sub")
LANES = 128
STEPS = 8
REC = 256
T = 8
PADY = 8


def split3(x):
    hi = x.astype(jnp.bfloat16)
    rest = x - hi.astype(jnp.float32)
    mid = rest.astype(jnp.bfloat16)
    lo = (rest - mid.astype(jnp.float32)).astype(jnp.bfloat16)
    return hi, mid, lo


def dot3(onehot, x, dims):
    total = None
    for part in reversed(split3(x)):
        term = lax.dot_general(onehot, part, (dims, ((), ())), preferred_element_type=jnp.float32)
        total = term if total is None else total + term
    return total


def paired(ref):
    n = ref.shape[0] // 2
    return jnp.concatenate([ref[pl.ds(0, n, stride=2), :], ref[pl.ds(1, n, stride=2), :]], axis=1)


def pick_kernel(near_ref, x_ref, out_ref):
    x = paired(x_ref)
    n = near_ref.shape[1] // 2
    near = lax.shift_right_arithmetic(near_ref[:, 0:n], 1)
    onehot = (lax.broadcasted_iota(jnp.int32, (x.shape[0], n), 0) == near).astype(jnp.bfloat16)
    picked = dot3(onehot, x, ((0,), (0,)))
    for half in range(2):
        out_ref[pl.ds(half, n, stride=2), :] = picked[:, half * LANES : (half + 1) * LANES]


def drop_kernel(wanted_ref, x_ref, out_ref):
    x = paired(x_ref)
    wanted = wanted_ref[...]
    slots = out_ref.shape[0] // 2
    onehot = (lax.broadcasted_iota(jnp.int32, (slots, wanted.shape[1]), 0) == wanted).astype(jnp.bfloat16)
    total = dot3(onehot, x, ((1,), (0,)))
    for half in range(2):
        out_ref[pl.ds(half, slots, stride=2), :] = total[:, half * LANES : (half + 1) * LANES]


def tile_half(speed3, block, half, ny):
    n = T * ny // 2
    value = speed3[pl.ds(2 * block + half, n, stride=6), :]
    return value.reshape(T // 2, ny, LANES)


def square_speed(dst, speed3, ny):
    for block in range(3):
        for half in range(2):
            value = tile_half(speed3, block, half, ny)
            first = block * T + half * (T // 2)
            dst[first : first + T // 2] = value * value


def each(lo, hi, body):
    for x in range(lo, hi):
        body(x, 0)


def bring(parts, ny, sems):
    copies = []
    for i, (src, dst, at) in enumerate(parts):
        place = dst.at[at : at + src.shape[0], PADY : PADY + ny, :]
        copies.append(pltpu.make_async_copy(src, place, sems.at[i]))
    for c in copies:
        c.start()
    return copies


def clear_edges(edge_ref, *fields):
    for i, at in ((0, 0), (1, 2 * T)):

        @pl.when(edge_ref[i] == 0)
        def _():
            for f in fields:
                f[at : at + T] = jnp.zeros((T,) + f.shape[1:], jnp.float32)


def clear_pad(dst, ny):
    zero = jnp.zeros((dst.shape[0], PADY, LANES), jnp.float32)
    dst[:, 0:PADY, :] = zero
    dst[:, PADY + ny : PADY + ny + PADY, :] = zero


def layer_laplace(cur, x, ny, first, last):
    mid = cur[x, PADY : PADY + ny, :]
    total = cur[x + 1, PADY : PADY + ny, :] + cur[x - 1, PADY : PADY + ny, :]
    total = total + cur[x, PADY + 1 : PADY + 1 + ny, :] + cur[x, PADY - 1 : PADY - 1 + ny, :]
    up = jnp.where(last, 0.0, pltpu.roll(mid, LANES - 1, 1))
    down = jnp.where(first, 0.0, pltpu.roll(mid, 1, 1))
    total = total + up + down
    return mid, total - 6.0 * mid


def forward_kernel(
    edge_ref, src_ref, wave_ref, rec_ref, obs_ref,
    speed3, low, po, co, high,
    lap_ref, res_ref, prev, cur, speed_sq, sems,
):
    ny = po.shape[1]
    rows = T * ny
    clear_pad(prev, ny)
    clear_pad(cur, ny)
    copies = bring(
        [
            (low.at[0:T], prev, 0), (po, prev, T), (high.at[0:T], prev, 2 * T),
            (low.at[T:], cur, 0), (co, cur, T), (high.at[T:], cur, 2 * T),
        ],
        ny,
        sems,
    )
    square_speed(speed_sq, speed3, ny)
    for c in copies:
        c.wait()
    clear_edges(edge_ref, prev, cur)
    lane = lax.broadcasted_iota(jnp.int32, (ny, LANES), 1)
    first, last = lane == 0, lane == LANES - 1
    src_x, src_y, src_z = src_ref[0], src_ref[1], src_ref[2]
    inside = (src_x >= 0) & (src_x < 3 * T)
    src_lane = lax.broadcasted_iota(jnp.int32, (1, LANES), 1) == src_z
    rec = rec_ref[...]
    onehot = (lax.broadcasted_iota(jnp.int32, (rows, REC), 0) == rec[0:1]).astype(jnp.bfloat16)
    z_mask = lax.broadcasted_iota(jnp.int32, (LANES, REC), 0) == rec[1:2]
    own = (rec[0:1] >= 0) & (rec[0:1] < rows)
    for n in range(STEPS):
        old, now = (prev, cur) if n % 2 == 0 else (cur, prev)

        def update(x, keep):
            mid, lap = layer_laplace(now, x, ny, first, last)
            old[x, PADY : PADY + ny, :] = (2.0 * mid - old[x, PADY : PADY + ny, :]) + speed_sq[x] * lap
            return lap

        def outer(x, carry):
            update(x, False)
            return carry

        def inner(x, carry):
            lap_ref[n, x - T] = update(x, True)
            return carry

        each(1 + n, T, outer)
        each(T, 2 * T, inner)
        each(2 * T, 3 * T - 1 - n, outer)

        @pl.when(inside)
        def _():
            row = pl.ds(src_y + PADY, 1)
            old[src_x, row, :] = old[src_x, row, :] + jnp.where(src_lane, wave_ref[n], 0.0)

        field = old[T : 2 * T, PADY : PADY + ny, :].reshape(rows, LANES)
        total = None
        for part in reversed(split3(field)):
            term = lax.dot_general(part, onehot, (((0,), (0,)), ((), ())), preferred_element_type=jnp.float32)
            total = term if total is None else total + term
        sample = jnp.sum(jnp.where(z_mask, total, 0.0), axis=0, keepdims=True)
        res_ref[n : n + 1, :] = jnp.where(own, sample - obs_ref[n : n + 1, :], 0.0)


def adjoint_kernel(
    edge_ref, rec_ref, rl, ro, rh,
    speed3, low, po, co, high, lap_ref,
    out_ref, prev, cur, speed_sq, inject, speed, sems,
):
    ny = po.shape[1]
    clear_pad(prev, ny)
    clear_pad(cur, ny)
    copies = bring(
        [
            (low.at[0:T], prev, 0), (po, prev, T), (high.at[0:T], prev, 2 * T),
            (low.at[T:], cur, 0), (co, cur, T), (high.at[T:], cur, 2 * T),
        ],
        ny,
        sems,
    )
    square_speed(speed_sq, speed3, ny)
    lane = lax.broadcasted_iota(jnp.int32, (ny, LANES), 1)
    first, last = lane == 0, lane == LANES - 1
    for half in range(2):
        speed[half * (T // 2) : (half + 1) * (T // 2)] = tile_half(speed3, 1, half, ny)
    rec = rec_ref[...]
    resid = rl[...] + ro[...] + rh[...]
    z_mask = lax.broadcasted_iota(jnp.int32, (LANES, REC), 0) == rec[1:2]
    for c in copies:
        c.wait()
    clear_edges(edge_ref, prev, cur)
    for k in range(STEPS):
        old, now = (prev, cur) if k % 2 == 0 else (cur, prev)
        n = STEPS - 1 - k
        lo, hi = 1 + k, 3 * T - 1 - k
        span = (hi - lo) * ny
        onehot = (
            lax.broadcasted_iota(jnp.int32, (span, REC), 0) == rec[0:1] + (T - lo) * ny
        ).astype(jnp.bfloat16)
        spread = jnp.where(z_mask, resid[n : n + 1, :], 0.0)
        inject[lo:hi] = dot3(onehot, spread, ((1,), (1,))).reshape(hi - lo, ny, LANES)

        def update(x):
            mid, lap = layer_laplace(now, x, ny, first, last)
            new = (2.0 * mid - old[x, PADY : PADY + ny, :]) + speed_sq[x] * lap + inject[x]
            old[x, PADY : PADY + ny, :] = new
            return new

        def outer(x, carry):
            update(x)
            return carry

        def inner(x, carry):
            new = update(x)
            term = speed[x - T] * new * lap_ref[n, x - T]
            if k == 0:
                out_ref[x - T] = term
            elif k == STEPS - 1:
                out_ref[x - T] = (2.0 / STEPS) * (out_ref[x - T] + term)
            else:
                out_ref[x - T] = out_ref[x - T] + term
            return carry

        each(lo, T, outer)
        each(T, 2 * T, inner)
        each(2 * T, hi, outer)


def vmem():
    return pl.BlockSpec(memory_space=pltpu.VMEM)


def smem():
    return pl.BlockSpec(memory_space=pltpu.SMEM)


def anywhere():
    return pl.BlockSpec(memory_space=pl.ANY)


def params():
    return pltpu.CompilerParams(vmem_limit_bytes=48 * 1024 * 1024)


def call_pick(near, x):
    return pl.pallas_call(
        pick_kernel,
        out_shape=jax.ShapeDtypeStruct((near.shape[1], x.shape[1]), jnp.float32),
        in_specs=[vmem(), vmem()],
        out_specs=vmem(),
        compiler_params=params(),
    )(near, x)


def cut_kernel(x_ref, out_ref):
    k, n, _ = x_ref.shape
    for i in range(k):
        out_ref[pl.ds(i, n, stride=k), :] = x_ref[i]


def call_cut(x):
    return pl.pallas_call(
        cut_kernel,
        out_shape=jax.ShapeDtypeStruct((x.shape[0] * x.shape[1], x.shape[2]), jnp.float32),
        in_specs=[vmem()],
        out_specs=vmem(),
        compiler_params=params(),
    )(x)


def stack_kernel(*refs):
    fields, out, sems = refs[:-2], refs[-2], refs[-1]
    copies = [pltpu.make_async_copy(f, out.at[i * T : (i + 1) * T], sems.at[i]) for i, f in enumerate(fields)]
    for c in copies:
        c.start()
    for c in copies:
        c.wait()


def call_stack(*fields):
    return pl.pallas_call(
        stack_kernel,
        out_shape=jax.ShapeDtypeStruct((len(fields) * T,) + fields[0].shape[1:], jnp.float32),
        in_specs=[anywhere()] * len(fields),
        out_specs=anywhere(),
        scratch_shapes=[pltpu.SemaphoreType.DMA((len(fields),))],
        compiler_params=params(),
    )(*fields)


def call_forward(edge, src_place, wave, rec, obs, speed3, fields):
    layers, ny, nz = fields[1].shape
    field = pltpu.VMEM((3 * T, ny + 2 * PADY, nz), jnp.float32)
    flat = pltpu.VMEM((3 * T, ny, nz), jnp.float32)
    return pl.pallas_call(
        forward_kernel,
        out_shape=(
            jax.ShapeDtypeStruct((STEPS, layers, ny, nz), jnp.float32),
            jax.ShapeDtypeStruct((STEPS, REC), jnp.float32),
        ),
        in_specs=[smem()] * 3 + [vmem()] * 3 + [anywhere()] * 4,
        out_specs=(vmem(), vmem()),
        scratch_shapes=[field, field, flat, pltpu.SemaphoreType.DMA((6,))],
        compiler_params=params(),
    )(edge, src_place, wave, rec, obs, speed3, *fields)


def call_adjoint(edge, rec, res3, speed3, fields, laps):
    layers, ny, nz = fields[1].shape
    field = pltpu.VMEM((3 * T, ny + 2 * PADY, nz), jnp.float32)
    flat = pltpu.VMEM((3 * T, ny, nz), jnp.float32)
    return pl.pallas_call(
        adjoint_kernel,
        out_shape=jax.ShapeDtypeStruct((layers, ny, nz), jnp.float32),
        in_specs=[smem()] + [vmem()] * 5 + [anywhere()] * 4 + [vmem()],
        out_specs=vmem(),
        scratch_shapes=[field, field, flat, flat, pltpu.VMEM((T, ny, nz), jnp.float32), pltpu.SemaphoreType.DMA((6,))],
        compiler_params=params(),
    )(edge, rec, *res3, speed3, *fields, laps)


def shards(
    velocity,
    tile_slot,
    anchors,
    source_cell,
    wavelet,
    receiver_cells,
    observed,
    fwd_prev,
    fwd_curr,
    adj_prev,
    adj_curr,
):
    n_shot = lax.axis_size("shot")
    n_sub = lax.axis_size("sub")
    n_all = n_shot * n_sub
    sub_index = lax.axis_index("sub")
    local_slots, layers, ny, nz = velocity.shape
    rows = layers * ny
    piece = rows // n_all
    forward = [(i, (i + 1) % n_sub) for i in range(n_sub)]
    backward = [(j, i) for i, j in forward]

    def both(x):
        return lax.ppermute(x, "sub", forward), lax.ppermute(x, "sub", backward)

    tiles = ((anchors[:, 0:1] + jnp.arange(n_sub, dtype=jnp.int32)) * n_shot + anchors[:, 1:2]).reshape(-1)
    table = jnp.arange(tile_slot.shape[0], dtype=jnp.int32)
    wanted = jnp.sum(jnp.where(table[:, None] == tiles[None, :], tile_slot[:, None], 0), axis=0)
    pad = jnp.pad(wanted.reshape(n_shot, n_sub), ((0, 0), (1, 1)), constant_values=-1)
    near = jnp.stack([pad[:, :-2], pad[:, 1:-1], pad[:, 2:]], axis=-1)
    half = jnp.arange(piece, dtype=jnp.int32)[:, None, None, None]
    near = jnp.where(near >= 0, near * piece + half, -1).reshape(1, n_all * 3 * piece)
    wanted = wanted.reshape(1, n_all)
    edge = jnp.stack([sub_index > 0, sub_index < n_sub - 1]).astype(jnp.int32)

    cells = receiver_cells[0]
    rec = jnp.stack([cells // nz - sub_index * rows, cells % nz])
    src = source_cell[0]
    src_place = jnp.stack([src // (ny * nz) - (sub_index - 1) * layers, src // nz % ny, src % nz])

    with jax.named_scope("halo_fields"):
        low, high = both(call_stack(fwd_prev[0], fwd_curr[0]))
        adj_low, adj_high = both(call_stack(adj_prev[0], adj_curr[0]))
    with jax.named_scope("spread_velocity"):
        cut = call_cut(velocity.reshape(local_slots * piece, n_all, nz))
        spread = lax.all_to_all(cut.reshape(n_all, local_slots, piece, nz), ALL, 0, 0, tiled=True)
    with jax.named_scope("pick_velocity"):
        picked = call_pick(near, spread.reshape(n_all * local_slots * piece, nz))
        picked, low, high = lax.optimization_barrier((picked, low, high))
    with jax.named_scope("deliver_velocity"):
        speed3 = lax.all_to_all(picked.reshape(n_all, 3, piece, nz), ALL, 0, 0, tiled=True)
        speed3 = speed3.reshape(n_all * 3 * piece, nz)

    fwd4 = (low, fwd_prev[0], fwd_curr[0], high)
    adj4 = (adj_low, adj_prev[0], adj_curr[0], adj_high)
    with jax.named_scope("forward"):
        laps, resid = call_forward(edge, src_place, wavelet[0], rec, observed[0], speed3, fwd4)
    with jax.named_scope("residuals"):
        res_low, res_high = both(resid)
        res3 = (res_low, resid, res_high)
    with jax.named_scope("adjoint"):
        image = call_adjoint(edge, rec, res3, speed3, adj4, laps)

    with jax.named_scope("spread_gradient"):
        pieces = lax.all_to_all(image.reshape(n_all, piece, nz), ALL, 0, 0, tiled=True)
    with jax.named_scope("drop_gradient"):
        dropped = pl.pallas_call(
            drop_kernel,
            out_shape=jax.ShapeDtypeStruct((n_all * local_slots * piece, nz), jnp.float32),
            in_specs=[vmem(), vmem()],
            out_specs=vmem(),
            compiler_params=params(),
        )(wanted, pieces.reshape(n_all * piece, nz))
    with jax.named_scope("deliver_gradient"):
        back = lax.all_to_all(dropped.reshape(n_all, local_slots * piece, nz), ALL, 0, 0, tiled=True)
        back = back.reshape(n_all, local_slots, piece, nz).transpose(1, 0, 2, 3)
    return back.reshape(velocity.shape)


def solution(mesh):
    return jax.shard_map(
        shards,
        mesh=mesh,
        in_specs=(
            P(("shot", "sub"), None, None, None),
            P(),
            P(),
            P("shot"),
            P("shot", None),
            P("shot", None),
            P("shot", None, None),
            P("shot", "sub", None, None),
            P("shot", "sub", None, None),
            P("shot", "sub", None, None),
            P("shot", "sub", None, None),
        ),
        out_specs=P(("shot", "sub"), None, None, None),
        check_vma=False,
    )
```

```python
import functools

import jax
import jax.numpy as jnp
from jax import lax
from jax.experimental import pallas as pl
from jax.experimental.pallas import tpu as pltpu
from jax.sharding import PartitionSpec as P

ALL = ("shot", "sub")
LANES = 128
STEPS = 8
REC = 256
T = 8
PADY = 8


def split3(x):
    hi = x.astype(jnp.bfloat16)
    rest = x - hi.astype(jnp.float32)
    mid = rest.astype(jnp.bfloat16)
    lo = (rest - mid.astype(jnp.float32)).astype(jnp.bfloat16)
    return hi, mid, lo


def dot3(onehot, x, dims):
    total = None
    for part in reversed(split3(x)):
        term = lax.dot_general(onehot, part, (dims, ((), ())), preferred_element_type=jnp.float32)
        total = term if total is None else total + term
    return total


def paired(ref):
    n = ref.shape[0] // 2
    return jnp.concatenate([ref[pl.ds(0, n, stride=2), :], ref[pl.ds(1, n, stride=2), :]], axis=1)


def pick_kernel(near_ref, x_ref, out_ref):
    x = paired(x_ref)
    n = near_ref.shape[1] // 2
    near = lax.shift_right_arithmetic(near_ref[:, 0:n], 1)
    onehot = (lax.broadcasted_iota(jnp.int32, (x.shape[0], n), 0) == near).astype(jnp.bfloat16)
    picked = dot3(onehot, x, ((0,), (0,)))
    for half in range(2):
        out_ref[pl.ds(half, n, stride=2), :] = picked[:, half * LANES : (half + 1) * LANES]


def drop_kernel(wanted_ref, x_ref, out_ref):
    x = paired(x_ref)
    wanted = wanted_ref[...]
    slots = out_ref.shape[0] // 2
    onehot = (lax.broadcasted_iota(jnp.int32, (slots, wanted.shape[1]), 0) == wanted).astype(jnp.bfloat16)
    total = dot3(onehot, x, ((1,), (0,)))
    for half in range(2):
        out_ref[pl.ds(half, slots, stride=2), :] = total[:, half * LANES : (half + 1) * LANES]


def tile_half(speed3, block, half, ny):
    n = T * ny // 2
    value = speed3[pl.ds(2 * block + half, n, stride=6), :]
    return value.reshape(T // 2, ny, LANES)


def square_speed(dst, speed3, ny):
    for block in range(3):
        for half in range(2):
            value = tile_half(speed3, block, half, ny)
            first = block * T + half * (T // 2)
            dst[first : first + T // 2] = value * value


def each(lo, hi, body):
    for x in range(lo, hi):
        body(x, 0)


def bring(parts, ny, sems):
    copies = []
    for i, (src, dst, at) in enumerate(parts):
        place = dst.at[at : at + src.shape[0], PADY : PADY + ny, :]
        copies.append(pltpu.make_async_copy(src, place, sems.at[i]))
    for c in copies:
        c.start()
    return copies


def clear_edges(edge_ref, *fields):
    for i, at in ((0, 0), (1, 2 * T)):

        @pl.when(edge_ref[i] == 0)
        def _():
            for f in fields:
                f[at : at + T] = jnp.zeros((T,) + f.shape[1:], jnp.float32)


def clear_pad(dst, ny):
    zero = jnp.zeros((dst.shape[0], PADY, LANES), jnp.float32)
    dst[:, 0:PADY, :] = zero
    dst[:, PADY + ny : PADY + ny + PADY, :] = zero


def layer_laplace(cur, x, ny, first, last):
    mid = cur[x, PADY : PADY + ny, :]
    total = cur[x + 1, PADY : PADY + ny, :] + cur[x - 1, PADY : PADY + ny, :]
    total = total + cur[x, PADY + 1 : PADY + 1 + ny, :] + cur[x, PADY - 1 : PADY - 1 + ny, :]
    up = jnp.where(last, 0.0, pltpu.roll(mid, LANES - 1, 1))
    down = jnp.where(first, 0.0, pltpu.roll(mid, 1, 1))
    total = total + up + down
    return mid, total - 6.0 * mid


def forward_kernel(
    edge_ref, src_ref, wave_ref, rec_ref, obs_ref,
    speed3, low, po, co, high,
    lap_ref, res_ref, prev, cur, speed_sq, sems,
):
    ny = po.shape[1]
    rows = T * ny
    clear_pad(prev, ny)
    clear_pad(cur, ny)
    copies = bring(
        [
            (low.at[0:T], prev, 0), (po, prev, T), (high.at[0:T], prev, 2 * T),
            (low.at[T:], cur, 0), (co, cur, T), (high.at[T:], cur, 2 * T),
        ],
        ny,
        sems,
    )
    square_speed(speed_sq, speed3, ny)
    for c in copies:
        c.wait()
    clear_edges(edge_ref, prev, cur)
    lane = lax.broadcasted_iota(jnp.int32, (ny, LANES), 1)
    first, last = lane == 0, lane == LANES - 1
    src_x, src_y, src_z = src_ref[0], src_ref[1], src_ref[2]
    inside = (src_x >= 0) & (src_x < 3 * T)
    src_lane = lax.broadcasted_iota(jnp.int32, (1, LANES), 1) == src_z
    rec = rec_ref[...]
    onehot = (lax.broadcasted_iota(jnp.int32, (rows, REC), 0) == rec[0:1]).astype(jnp.bfloat16)
    z_mask = lax.broadcasted_iota(jnp.int32, (LANES, REC), 0) == rec[1:2]
    own = (rec[0:1] >= 0) & (rec[0:1] < rows)
    for n in range(STEPS):
        old, now = (prev, cur) if n % 2 == 0 else (cur, prev)

        def update(x, keep):
            mid, lap = layer_laplace(now, x, ny, first, last)
            old[x, PADY : PADY + ny, :] = (2.0 * mid - old[x, PADY : PADY + ny, :]) + speed_sq[x] * lap
            return lap

        def outer(x, carry):
            update(x, False)
            return carry

        def inner(x, carry):
            lap_ref[n, x - T] = update(x, True)
            return carry

        each(1 + n, T, outer)
        each(T, 2 * T, inner)
        each(2 * T, 3 * T - 1 - n, outer)

        @pl.when(inside)
        def _():
            row = pl.ds(src_y + PADY, 1)
            old[src_x, row, :] = old[src_x, row, :] + jnp.where(src_lane, wave_ref[n], 0.0)

        field = old[T : 2 * T, PADY : PADY + ny, :].reshape(rows, LANES)
        total = None
        for part in reversed(split3(field)):
            term = lax.dot_general(part, onehot, (((0,), (0,)), ((), ())), preferred_element_type=jnp.float32)
            total = term if total is None else total + term
        sample = jnp.sum(jnp.where(z_mask, total, 0.0), axis=0, keepdims=True)
        res_ref[n : n + 1, :] = jnp.where(own, sample - obs_ref[n : n + 1, :], 0.0)


def adjoint_kernel(
    edge_ref, rec_ref, rl, ro, rh,
    speed3, low, po, co, high, lap_ref,
    out_ref, prev, cur, speed_sq, inject, speed, sems,
):
    ny = po.shape[1]
    clear_pad(prev, ny)
    clear_pad(cur, ny)
    copies = bring(
        [
            (low.at[0 : T - 1], prev, 1), (po, prev, T), (high.at[0 : T - 1], prev, 2 * T),
            (low.at[T - 1 :], cur, 0), (co, cur, T), (high.at[T - 1 :], cur, 2 * T),
        ],
        ny,
        sems,
    )
    square_speed(speed_sq, speed3, ny)
    lane = lax.broadcasted_iota(jnp.int32, (ny, LANES), 1)
    first, last = lane == 0, lane == LANES - 1
    for half in range(2):
        speed[half * (T // 2) : (half + 1) * (T // 2)] = tile_half(speed3, 1, half, ny)
    rec = rec_ref[...]
    resid = rl[...] + ro[...] + rh[...]
    z_mask = lax.broadcasted_iota(jnp.int32, (LANES, REC), 0) == rec[1:2]
    for c in copies:
        c.wait()
    clear_edges(edge_ref, prev, cur)
    for k in range(STEPS):
        old, now = (prev, cur) if k % 2 == 0 else (cur, prev)
        n = STEPS - 1 - k
        lo, hi = 1 + k, 3 * T - 1 - k
        span = (hi - lo) * ny
        onehot = (
            lax.broadcasted_iota(jnp.int32, (span, REC), 0) == rec[0:1] + (T - lo) * ny
        ).astype(jnp.bfloat16)
        spread = jnp.where(z_mask, resid[n : n + 1, :], 0.0)
        inject[lo:hi] = dot3(onehot, spread, ((1,), (1,))).reshape(hi - lo, ny, LANES)

        def update(x):
            mid, lap = layer_laplace(now, x, ny, first, last)
            new = (2.0 * mid - old[x, PADY : PADY + ny, :]) + speed_sq[x] * lap + inject[x]
            old[x, PADY : PADY + ny, :] = new
            return new

        def outer(x, carry):
            update(x)
            return carry

        def inner(x, carry):
            new = update(x)
            term = speed[x - T] * new * lap_ref[n, x - T]
            if k == 0:
                out_ref[x - T] = term
            elif k == STEPS - 1:
                out_ref[x - T] = (2.0 / STEPS) * (out_ref[x - T] + term)
            else:
                out_ref[x - T] = out_ref[x - T] + term
            return carry

        each(lo, T, outer)
        each(T, 2 * T, inner)
        each(2 * T, hi, outer)


def vmem():
    return pl.BlockSpec(memory_space=pltpu.VMEM)


def smem():
    return pl.BlockSpec(memory_space=pltpu.SMEM)


def anywhere():
    return pl.BlockSpec(memory_space=pl.ANY)


def params():
    return pltpu.CompilerParams(vmem_limit_bytes=48 * 1024 * 1024)


def call_pick(near, x):
    return pl.pallas_call(
        pick_kernel,
        out_shape=jax.ShapeDtypeStruct((near.shape[1], x.shape[1]), jnp.float32),
        in_specs=[vmem(), vmem()],
        out_specs=vmem(),
        compiler_params=params(),
    )(near, x)


def cut_kernel(x_ref, out_ref):
    k, n, _ = x_ref.shape
    for i in range(k):
        out_ref[pl.ds(i, n, stride=k), :] = x_ref[i]


def call_cut(x):
    return pl.pallas_call(
        cut_kernel,
        out_shape=jax.ShapeDtypeStruct((x.shape[0] * x.shape[1], x.shape[2]), jnp.float32),
        in_specs=[vmem()],
        out_specs=vmem(),
        compiler_params=params(),
    )(x)


def stack_kernel(first, count, *refs):
    fields, out, sems = refs[:-2], refs[-2], refs[-1]
    copies = []
    for i, field in enumerate(fields):
        at, part = (0, field.at[first : first + count]) if i == 0 else (count + (i - 1) * T, field)
        copies.append(pltpu.make_async_copy(part, out.at[at : at + part.shape[0]], sems.at[i]))
    for c in copies:
        c.start()
    for c in copies:
        c.wait()


def call_stack(first, count, *fields):
    layers = count + (len(fields) - 1) * T
    return pl.pallas_call(
        functools.partial(stack_kernel, first, count),
        out_shape=jax.ShapeDtypeStruct((layers,) + fields[0].shape[1:], jnp.float32),
        in_specs=[anywhere()] * len(fields),
        out_specs=anywhere(),
        scratch_shapes=[pltpu.SemaphoreType.DMA((len(fields),))],
        compiler_params=params(),
    )(*fields)


def call_forward(edge, src_place, wave, rec, obs, speed3, fields):
    layers, ny, nz = fields[1].shape
    field = pltpu.VMEM((3 * T, ny + 2 * PADY, nz), jnp.float32)
    flat = pltpu.VMEM((3 * T, ny, nz), jnp.float32)
    return pl.pallas_call(
        forward_kernel,
        out_shape=(
            jax.ShapeDtypeStruct((STEPS, layers, ny, nz), jnp.float32),
            jax.ShapeDtypeStruct((STEPS, REC), jnp.float32),
        ),
        in_specs=[smem()] * 3 + [vmem()] * 3 + [anywhere()] * 4,
        out_specs=(vmem(), vmem()),
        scratch_shapes=[field, field, flat, pltpu.SemaphoreType.DMA((6,))],
        compiler_params=params(),
    )(edge, src_place, wave, rec, obs, speed3, *fields)


def call_adjoint(edge, rec, res3, speed3, fields, laps):
    layers, ny, nz = fields[1].shape
    field = pltpu.VMEM((3 * T, ny + 2 * PADY, nz), jnp.float32)
    flat = pltpu.VMEM((3 * T, ny, nz), jnp.float32)
    return pl.pallas_call(
        adjoint_kernel,
        out_shape=jax.ShapeDtypeStruct((layers, ny, nz), jnp.float32),
        in_specs=[smem()] + [vmem()] * 5 + [anywhere()] * 4 + [vmem()],
        out_specs=vmem(),
        scratch_shapes=[field, field, flat, flat, pltpu.VMEM((T, ny, nz), jnp.float32), pltpu.SemaphoreType.DMA((6,))],
        compiler_params=params(),
    )(edge, rec, *res3, speed3, *fields, laps)


def shards(
    velocity,
    tile_slot,
    anchors,
    source_cell,
    wavelet,
    receiver_cells,
    observed,
    fwd_prev,
    fwd_curr,
    adj_prev,
    adj_curr,
):
    n_shot = lax.axis_size("shot")
    n_sub = lax.axis_size("sub")
    n_all = n_shot * n_sub
    sub_index = lax.axis_index("sub")
    local_slots, layers, ny, nz = velocity.shape
    rows = layers * ny
    piece = rows // n_all
    forward = [(i, (i + 1) % n_sub) for i in range(n_sub)]
    backward = [(j, i) for i, j in forward]

    def both(up, down):
        return lax.ppermute(up, "sub", forward), lax.ppermute(down, "sub", backward)

    tiles = ((anchors[:, 0:1] + jnp.arange(n_sub, dtype=jnp.int32)) * n_shot + anchors[:, 1:2]).reshape(-1)
    table = jnp.arange(tile_slot.shape[0], dtype=jnp.int32)
    wanted = jnp.sum(jnp.where(table[:, None] == tiles[None, :], tile_slot[:, None], 0), axis=0)
    pad = jnp.pad(wanted.reshape(n_shot, n_sub), ((0, 0), (1, 1)), constant_values=-1)
    near = jnp.stack([pad[:, :-2], pad[:, 1:-1], pad[:, 2:]], axis=-1)
    half = jnp.arange(piece, dtype=jnp.int32)[:, None, None, None]
    near = jnp.where(near >= 0, near * piece + half, -1).reshape(1, n_all * 3 * piece)
    wanted = wanted.reshape(1, n_all)
    edge = jnp.stack([sub_index > 0, sub_index < n_sub - 1]).astype(jnp.int32)

    cells = receiver_cells[0]
    rec = jnp.stack([cells // nz - sub_index * rows, cells % nz])
    src = source_cell[0]
    src_place = jnp.stack([src // (ny * nz) - (sub_index - 1) * layers, src // nz % ny, src % nz])

    with jax.named_scope("halo_fields"):
        low, high = both(*[call_stack(0, T, fwd_prev[0], fwd_curr[0])] * 2)
        adj_low, adj_high = both(*(call_stack(first, T - 1, adj_prev[0], adj_curr[0]) for first in (1, 0)))
    with jax.named_scope("spread_velocity"):
        cut = call_cut(velocity.reshape(local_slots * piece, n_all, nz))
        spread = lax.all_to_all(cut.reshape(n_all, local_slots, piece, nz), ALL, 0, 0, tiled=True)
    with jax.named_scope("pick_velocity"):
        picked = call_pick(near, spread.reshape(n_all * local_slots * piece, nz))
        picked, low, high = lax.optimization_barrier((picked, low, high))
    with jax.named_scope("deliver_velocity"):
        speed3 = lax.all_to_all(picked.reshape(n_all, 3, piece, nz), ALL, 0, 0, tiled=True)
        speed3 = speed3.reshape(n_all * 3 * piece, nz)

    fwd4 = (low, fwd_prev[0], fwd_curr[0], high)
    adj4 = (adj_low, adj_prev[0], adj_curr[0], adj_high)
    with jax.named_scope("forward"):
        laps, resid = call_forward(edge, src_place, wavelet[0], rec, observed[0], speed3, fwd4)
    with jax.named_scope("residuals"):
        res_low, res_high = both(resid, resid)
        res3 = (res_low, resid, res_high)
    with jax.named_scope("adjoint"):
        image = call_adjoint(edge, rec, res3, speed3, adj4, laps)

    with jax.named_scope("spread_gradient"):
        pieces = lax.all_to_all(image.reshape(n_all, piece, nz), ALL, 0, 0, tiled=True)
    with jax.named_scope("drop_gradient"):
        dropped = pl.pallas_call(
            drop_kernel,
            out_shape=jax.ShapeDtypeStruct((n_all * local_slots * piece, nz), jnp.float32),
            in_specs=[vmem(), vmem()],
            out_specs=vmem(),
            compiler_params=params(),
        )(wanted, pieces.reshape(n_all * piece, nz))
    with jax.named_scope("deliver_gradient"):
        back = lax.all_to_all(dropped.reshape(n_all, local_slots * piece, nz), ALL, 0, 0, tiled=True)
        back = back.reshape(n_all, local_slots, piece, nz).transpose(1, 0, 2, 3)
    return back.reshape(velocity.shape)


def solution(mesh):
    return jax.shard_map(
        shards,
        mesh=mesh,
        in_specs=(
            P(("shot", "sub"), None, None, None),
            P(),
            P(),
            P("shot"),
            P("shot", None),
            P("shot", None),
            P("shot", None, None),
            P("shot", "sub", None, None),
            P("shot", "sub", None, None),
            P("shot", "sub", None, None),
            P("shot", "sub", None, None),
        ),
        out_specs=P(("shot", "sub"), None, None, None),
        check_vma=False,
    )
```
